32 devices in a mesh: section: 8 (over z, x), dp: 4 (over y, core).
Axes of the slice: x: 2, y: 2, z: 4, core: 2. Of those that a mesh axis runs over, the one named last changes fastest.
Arguments:
- stream_in: bfloat16 [1024, 2048], P('dp'), may hold values from -6 to 6
- sample_ids: int32 [4, 8], P('dp'), may hold values from 0 to 31
- epoch_buffer: bfloat16 [8, 128, 32, 2048], P('section', 'dp'), may hold values from -8 to 8
- layer_weight: bfloat16 [8, 2048, 2048], P('section', 'dp'), may hold values from -0.125 to 0.125
- top_cotangent: bfloat16 [1024, 2048], P('dp'), may hold values from -6 to 6
Outputs:
- decoded: bfloat16 [8, 1024, 2048], P('section', 'dp')
- weight_grad: float32 [8, 2048, 2048], P('section', 'dp')
The draws below stay inside these ranges and needn't reach their ends.
Inputs may be any that keep to these rules, and one draw needn't show every extreme that they name: `sample_ids`: an entry of the replica's own pool of 32 samples.
All inputs are finite; a program needn't handle non-finite values.
Results may differ from the reference program's by a relative error of at most 0.035.
Values may be sent and summed in bfloat16 or wider, within the bound.
A program may use at most 128 MiB of HBM per device.

```python
import jax
import jax.numpy as jnp
from jax import lax

D = 2048
SECTIONS = 8
MB = 8
TOK_MB = 32
POOL = 32
ROWS = 1024
N_DP = 4


def touch_ends(result, rng, low, top_value):
    longest = result.shape.index(max(result.shape))
    spots = []
    for shift in (0, 1):
        where = [jax.random.randint(jax.random.fold_in(rng, axis), (), 0, length) for axis, length in enumerate(result.shape)]
        where[longest] = (where[longest] + shift) % result.shape[longest]
        spots.append(tuple(where))
    return result.at[spots[0]].set(low).at[spots[1]].set(top_value)


def block_levels(own_key, dims, cuts, smallest, top_value):
    factor_of = 1.0
    for dim, blocks in cuts:
        steps = jax.random.uniform(jax.random.fold_in(jax.random.fold_in(own_key, 6), dim), (blocks,), jnp.float32, smallest / len(cuts), top_value / len(cuts))
        factor_of = factor_of * jnp.repeat(jnp.exp(steps), dims[dim] // blocks).reshape((-1,) + (1,) * (len(dims) - 1 - dim))
    return factor_of


def normal_values(rng, shape, deviation, limit, shards=(), kind=jnp.bfloat16):
    result = jax.random.normal(rng, shape, jnp.float32) * deviation
    if len(shards) > 0:
        result = block_levels(rng, shape, shards, -0.22, 0.18) * result
    return jnp.clip(result, min=-limit, max=limit).astype(kind)


def setup_inputs(seed: int = 0) -> dict:
    seeds = jax.random.split(jax.random.key(seed), 6)
    stream_in = normal_values(seeds[0], (ROWS, D), 1.0, 6.0, ((0, 4),))
    sample_ids = touch_ends(jax.random.randint(seeds[1], (N_DP, MB), 0, POOL), jax.random.fold_in(seeds[1], 1), 0, POOL - 1).astype(jnp.int32)
    epoch_buffer = normal_values(seeds[2], (SECTIONS, N_DP * POOL, TOK_MB, D), 1.5, 8.0, ((0, 8), (1, 4)))
    layer_weight = normal_values(seeds[3], (SECTIONS, D, D), D ** -0.5, 0.125, ((0, 8), (1, 4)))
    top_cotangent = normal_values(seeds[4], (ROWS, D), 1.0, 6.0, ((0, 4),))
    return dict(stream_in=stream_in, sample_ids=sample_ids, epoch_buffer=epoch_buffer, layer_weight=layer_weight, top_cotangent=top_cotangent)


epsilon = 1e-05

def normalize(values):
    return values * lax.rsqrt(lax.optimization_barrier(jnp.mean(values * values, axis=-1, keepdims=True)) + epsilon)

def encode(output_rows, base_rows):
    bound_rows = 2.0 * jnp.sqrt(lax.optimization_barrier(jnp.mean(output_rows * output_rows, axis=-1, keepdims=True)) + epsilon)
    delta_rows = jnp.clip(output_rows - base_rows, -bound_rows, bound_rows).astype(jnp.bfloat16)
    return (base_rows + delta_rows.astype(jnp.float32)).astype(jnp.bfloat16)

def reference(stream_in, sample_ids, epoch_buffer, layer_weight, top_cotangent):
    replicas = sample_ids.shape[0]
    replica_rows = jnp.arange(replicas, dtype=jnp.int32)[:, None]
    current = stream_in
    inputs_kept = []
    decoded_all = []
    for layer in range(SECTIONS):
        stored = epoch_buffer[layer].reshape(replicas, POOL, TOK_MB, D)
        base_rows = stored[replica_rows, sample_ids].reshape(-1, D).astype(jnp.float32)
        inputs_kept.append(current)
        values = current.astype(jnp.float32)
        normed = normalize(values).astype(jnp.bfloat16)
        output_rows = values + jnp.dot(normed, layer_weight[layer], preferred_element_type=jnp.float32)
        current = encode(output_rows, base_rows)
        decoded_all.append(current)
    cotangent = top_cotangent
    gradients = [None] * SECTIONS
    for layer in range(SECTIONS - 1, -1, -1):
        values = inputs_kept[layer].astype(jnp.float32)
        normed = normalize(values).astype(jnp.bfloat16)
        per_replica = jnp.einsum('rti,rto->rio', normed.reshape(replicas, -1, D).astype(jnp.float32), cotangent.reshape(replicas, -1, D).astype(jnp.float32), precision=lax.Precision.HIGHEST)
        rounded = lax.optimization_barrier(per_replica.astype(jnp.bfloat16))
        gradients[layer] = lax.optimization_barrier(jnp.sum(rounded.astype(jnp.float32), axis=0))
        backward_rows = lax.dot_general(cotangent, layer_weight[layer], (((1,), (1,)), ((), ())), preferred_element_type=jnp.float32)
        through = jax.vjp(normalize, values)[1](backward_rows)[0]
        cotangent = (cotangent.astype(jnp.float32) + through).astype(jnp.bfloat16)
    return (jnp.stack(decoded_all), jnp.stack(gradients))
```

```python
import functools

import jax
import jax.numpy as jnp
from jax import lax
from jax.experimental import pallas as pl
from jax.experimental.pallas import tpu as pltpu
from jax.sharding import PartitionSpec as P

epsilon = 1e-05
CHUNKS = 4
TILE = 512


def relay_kernel(sections, replicas, blocks, base_ref, stream_ref, weight_ref, top_ref,
                 decoded_ref, normed_all, cot_all,
                 weight, rows_in, normed, cot_in, cot_out, product,
                 load_sem, w_send, w_recv, w_side_send, w_side_recv,
                 x_send, x_recv, g_send, g_recv, n_send, n_recv,
                 c_send, c_recv, c_side_send, c_side_recv, own_sem):
    s = lax.axis_index("section")
    me = lax.axis_index("dp")
    last = sections - 1
    chips = replicas // 2
    chip, core = me // 2, lax.rem(me, 2)
    sibling = chip * 2 + 1 - core
    total, width = rows_in.shape
    step_rows = total // blocks
    shard = weight_ref.shape[0]
    piece = shard // CHUNKS
    after, before = lax.rem(s + 1, sections), lax.rem(s + last, sections)

    def peer(offset):
        return lax.rem(chip + offset, chips) * 2 + core

    def source(offset):
        return lax.rem(chip + chips - offset, chips) * 2

    def block(m):
        return pl.ds(pl.multiple_of(m * step_rows, step_rows), step_rows)

    def remote(src, dst, send, recv, **where):
        return pltpu.make_async_remote_copy(
            src_ref=src, dst_ref=dst, send_sem=send, recv_sem=recv,
            device_id=where, device_id_type=pl.DeviceIdType.MESH)

    barrier = pltpu.get_barrier_semaphore()

    def greet(**where):
        pl.semaphore_signal(barrier, inc=1, device_id=where, device_id_type=pl.DeviceIdType.MESH)

    for offset in range(1, replicas):
        greet(dp=lax.rem(me + offset, replicas))

    @pl.when(s < last)
    def _():
        greet(section=after)

    @pl.when(s > 0)
    def _():
        greet(section=before)

    stream_load = pltpu.make_async_copy(stream_ref, rows_in, load_sem.at[0])
    top_load = pltpu.make_async_copy(top_ref, cot_in, load_sem.at[1])
    shard_load = pltpu.make_async_copy(
        weight_ref, weight.at[pl.ds(pl.multiple_of(me * shard, shard), shard)], load_sem.at[2])
    shard_load.start()

    @pl.when(s == 0)
    def _():
        stream_load.start()

    @pl.when(s == last)
    def _():
        top_load.start()

    pl.semaphore_wait(
        barrier, replicas - 1 + jnp.minimum(s, 1) + jnp.minimum(last - s, 1))

    def weight_rows(owner, q):
        return weight.at[pl.ds(pl.multiple_of(owner * shard + q * piece, piece), piece)]

    def weight_direct(offset, q):
        return remote(weight_ref.at[pl.ds(q * piece, piece)], weight_rows(me, q),
                      w_send.at[offset - 1, q], w_recv.at[offset - 1, q], dp=peer(offset))

    def weight_side(offset, q):
        if offset == 0:
            src = weight_ref.at[pl.ds(q * piece, piece)]
        else:
            src = weight_rows(source(offset) + core, q)
        return remote(src, weight_rows(source(offset) + core, q),
                      w_side_send.at[offset, q], w_side_recv.at[offset, q], dp=sibling)

    for q in range(CHUNKS):
        for offset in range(1, chips):
            weight_direct(offset, q).start()
        weight_side(0, q).start()
    for q in range(CHUNKS):
        for offset in range(1, chips):
            weight_direct(offset, q).wait_recv()
            weight_side(offset, q).start()
    shard_load.wait()
    for q in range(CHUNKS):
        for offset in range(chips):
            weight_side(offset, q).wait_recv()

    @pl.when(s == 0)
    def _():
        stream_load.wait()

    @pl.when(s == last)
    def _():
        top_load.wait()

    def send_rows(m):
        return remote(decoded_ref.at[block(m)], rows_in.at[block(m)],
                      x_send.at[m], x_recv.at[m], section=after)

    def send_cot(m):
        return remote(cot_out.at[block(m)], cot_in.at[block(m)],
                      g_send.at[m], g_recv.at[m], section=before)

    def send_normed(offset):
        other = lax.rem(me + offset, replicas)
        return remote(normed.at[:, pl.ds(pl.multiple_of(other * shard, shard), shard)],
                      normed_all.at[pl.ds(pl.multiple_of(me * total, total), total)],
                      n_send.at[offset - 1], n_recv.at[offset - 1], dp=other)

    own_normed = pltpu.make_async_copy(
        normed.at[:, pl.ds(pl.multiple_of(me * shard, shard), shard)],
        normed_all.at[pl.ds(pl.multiple_of(me * total, total), total)], load_sem.at[3])

    def cot_rows(owner, m):
        return cot_all.at[pl.ds(pl.multiple_of(owner * total + m * step_rows, step_rows), step_rows)]

    def cot_direct(offset, m):
        return remote(cot_in.at[block(m)], cot_rows(me, m),
                      c_send.at[offset - 1, m], c_recv.at[offset - 1, m], dp=peer(offset))

    def cot_side(offset, m):
        owner = source(offset) + core
        src = cot_in.at[block(m)] if offset == 0 else cot_rows(owner, m)
        return remote(src, cot_rows(owner, m),
                      c_side_send.at[offset, m], c_side_recv.at[offset, m], dp=sibling)

    def cot_own(m):
        return pltpu.make_async_copy(cot_in.at[block(m)], cot_rows(me, m), own_sem.at[m])

    def relay(m):
        for offset in range(1, chips):
            cot_direct(offset, m).wait_recv()
            cot_side(offset, m).start()

    def forward(m):
        @pl.when(s > 0)
        def _():
            send_rows(m).wait_recv()

        values = rows_in[block(m), :].astype(jnp.float32)
        scale = lax.rsqrt(jnp.mean(values * values, axis=-1, keepdims=True) + epsilon)
        scaled = (values * scale).astype(jnp.bfloat16)
        normed[block(m), :] = scaled
        squares = jnp.zeros((step_rows, 1), jnp.float32)
        for start in range(0, width, TILE):
            part = rows_in[block(m), start:start + TILE].astype(jnp.float32) + jnp.dot(
                scaled, weight[:, start:start + TILE], preferred_element_type=jnp.float32)
            product[:, start:start + TILE] = part
            squares += jnp.sum(part * part, axis=-1, keepdims=True)
        bound = 2.0 * jnp.sqrt(squares / width + epsilon)
        base = base_ref[block(m), :].astype(jnp.float32)
        delta = jnp.clip(product[...] - base, -bound, bound).astype(jnp.bfloat16)
        decoded_ref[block(m), :] = (base + delta.astype(jnp.float32)).astype(jnp.bfloat16)

        @pl.when(s < last)
        def _():
            send_rows(m).start()

    def backward(m):
        @pl.when(s < last)
        def _():
            send_cot(m).wait_recv()

        cot_side(0, m).start()
        for offset in range(1, chips):
            cot_direct(offset, m).start()
        cot_own(m).start()

        @pl.when(s > 0)
        def _():
            values = rows_in[block(m), :].astype(jnp.float32)
            scale = lax.rsqrt(jnp.mean(values * values, axis=-1, keepdims=True) + epsilon)
            incoming = cot_in[block(m), :]
            along = jnp.zeros((step_rows, 1), jnp.float32)
            for start in range(0, width, TILE):
                part = lax.dot_general(incoming, weight[start:start + TILE, :],
                                       (((1,), (1,)), ((), ())), preferred_element_type=jnp.float32)
                product[:, start:start + TILE] = part
                along += jnp.sum(
                    part * rows_in[block(m), start:start + TILE].astype(jnp.float32),
                    axis=-1, keepdims=True)
            through = scale * (product[...] - values * (scale * scale * (along / width)))
            cot_out[block(m), :] = (incoming.astype(jnp.float32) + through).astype(jnp.bfloat16)
            send_cot(m).start()

        @pl.when(m > 0)
        def _():
            relay(m - 1)

    lag = jnp.minimum(blocks, ((last - s) * 5) // 2)

    def step(k, carry):
        @pl.when(k < blocks)
        def _():
            forward(k)

        @pl.when(k == blocks - 1)
        def _():
            own_normed.start()
            for offset in range(1, replicas):
                send_normed(offset).start()

        @pl.when((k >= lag) & (k < lag + blocks))
        def _():
            backward(k - lag)

        return carry

    lax.fori_loop(0, 2 * blocks, step, 0)
    relay(blocks - 1)

    own_normed.wait()
    for offset in range(1, replicas):
        send_normed(offset).wait_send()
        send_normed(offset).wait_recv()
    for q in range(CHUNKS):
        for offset in range(1, chips):
            weight_direct(offset, q).wait_send()
        for offset in range(chips):
            weight_side(offset, q).wait_send()

    def finish(m, carry):
        @pl.when(s < last)
        def _():
            send_rows(m).wait_send()

        @pl.when(s > 0)
        def _():
            send_cot(m).wait_send()

        cot_own(m).wait()
        for offset in range(1, chips):
            cot_direct(offset, m).wait_send()
        for offset in range(chips):
            cot_side(offset, m).wait_send()
            cot_side(offset, m).wait_recv()
        return carry

    lax.fori_loop(0, blocks, finish, 0)


def local(sections, replicas, stream_in, sample_ids, epoch_buffer, layer_weight, top_cotangent):
    total, width = stream_in.shape
    blocks = sample_ids.shape[1]
    shard = layer_weight.shape[1]
    chips = replicas // 2
    base = jnp.take(epoch_buffer[0], sample_ids[0], axis=0, mode="clip").reshape(total, width)
    dma = pltpu.SemaphoreType.DMA
    vmem = pl.BlockSpec(memory_space=pltpu.VMEM)
    anywhere = pl.BlockSpec(memory_space=pl.ANY)
    far = max(chips - 1, 1)
    decoded, normed_all, cot_all = pl.pallas_call(
        functools.partial(relay_kernel, sections, replicas, blocks),
        out_shape=(
            jax.ShapeDtypeStruct((total, width), jnp.bfloat16),
            jax.ShapeDtypeStruct((replicas * total, shard), jnp.bfloat16),
            jax.ShapeDtypeStruct((replicas * total, width), jnp.bfloat16),
        ),
        in_specs=[vmem, anywhere, anywhere, anywhere],
        out_specs=(vmem, anywhere, anywhere),
        scratch_shapes=[
            pltpu.VMEM((width, width), jnp.bfloat16),
            pltpu.VMEM((total, width), jnp.bfloat16),
            pltpu.VMEM((total, width), jnp.bfloat16),
            pltpu.VMEM((total, width), jnp.bfloat16),
            pltpu.VMEM((total, width), jnp.bfloat16),
            pltpu.VMEM((total // blocks, width), jnp.float32),
            dma((4,)),
            dma((far, CHUNKS)), dma((far, CHUNKS)), dma((chips, CHUNKS)), dma((chips, CHUNKS)),
            dma((blocks,)), dma((blocks,)), dma((blocks,)), dma((blocks,)),
            dma((replicas - 1,)), dma((replicas - 1,)),
            dma((far, blocks)), dma((far, blocks)), dma((chips, blocks)), dma((chips, blocks)),
            dma((blocks,)),
        ],
        compiler_params=pltpu.CompilerParams(
            collective_id=0, has_side_effects=True, vmem_limit_bytes=48 * 1024 * 1024),
    )(base, stream_in, layer_weight[0], top_cotangent)
    gradient = lax.dot_general(
        normed_all, cot_all, (((0,), (0,)), ((), ())), preferred_element_type=jnp.float32)
    return (decoded[None], gradient[None])


def solution(mesh):
    in_specs = (
        P("dp", None),
        P("dp", None),
        P("section", "dp", None, None),
        P("section", "dp", None),
        P("dp", None),
    )
    out_specs = (P("section", "dp", None), P("section", "dp", None))
    body = functools.partial(local, mesh.shape["section"], mesh.shape["dp"])
    return jax.shard_map(body, mesh=mesh, in_specs=in_specs, out_specs=out_specs, check_vma=False)
```

```python
import functools

import jax
import jax.numpy as jnp
from jax import lax
from jax.experimental import pallas as pl
from jax.experimental.pallas import tpu as pltpu
from jax.sharding import PartitionSpec as P

epsilon = 1e-05
CHUNKS = 4
TILE = 512
PIECES = 4


def relay_kernel(sections, replicas, blocks, ids_ref, epoch_ref, stream_ref, weight_whole, top_ref,
                 decoded_ref, normed_all, cot_all,
                 weight, rows_in, normed, cot_in, cot_out, product, ahead, epoch,
                 load_sem, w_send, w_recv, w_side_send, w_side_recv,
                 x_send, x_recv, g_send, g_recv, n_send, n_recv,
                 c_send, c_recv, c_side_send, c_side_recv, own_sem):
    s = lax.axis_index("section")
    me = lax.axis_index("dp")
    last = sections - 1
    chips = replicas // 2
    chip, core = me // 2, lax.rem(me, 2)
    sibling = chip * 2 + 1 - core
    total, width = rows_in.shape
    step_rows = total // blocks
    weight_ref = weight_whole.at[0]
    shard = weight_ref.shape[0]
    span = width // PIECES
    piece = shard // CHUNKS
    after, before = lax.rem(s + 1, sections), lax.rem(s + last, sections)

    def peer(offset):
        return lax.rem(chip + offset, chips) * 2 + core

    def source(offset):
        return lax.rem(chip + chips - offset, chips) * 2

    def block(m):
        return pl.ds(pl.multiple_of(m * step_rows, step_rows), step_rows)

    def remote(src, dst, send, recv, **where):
        return pltpu.make_async_remote_copy(
            src_ref=src, dst_ref=dst, send_sem=send, recv_sem=recv,
            device_id=where, device_id_type=pl.DeviceIdType.MESH)

    barrier = pltpu.get_barrier_semaphore()

    def greet(**where):
        pl.semaphore_signal(barrier, inc=1, device_id=where, device_id_type=pl.DeviceIdType.MESH)

    for offset in range(1, replicas):
        greet(dp=lax.rem(me + offset, replicas))

    @pl.when(s < last)
    def _():
        greet(section=after)

    @pl.when(s > 0)
    def _():
        greet(section=before)

    stream_load = pltpu.make_async_copy(stream_ref, rows_in, load_sem.at[0])
    top_load = pltpu.make_async_copy(top_ref, cot_in, load_sem.at[1])
    shard_load = pltpu.make_async_copy(
        weight_ref, weight.at[pl.ds(pl.multiple_of(me * shard, shard), shard)], load_sem.at[2])
    shard_load.start()
    epoch_load = pltpu.make_async_copy(epoch_ref.at[0], epoch, load_sem.at[4])

    @pl.when(s == 0)
    def _():
        stream_load.start()

    @pl.when(s == last)
    def _():
        top_load.start()

    pl.semaphore_wait(
        barrier, replicas - 1 + jnp.minimum(s, 1) + jnp.minimum(last - s, 1))

    def weight_rows(owner, q):
        return weight.at[pl.ds(pl.multiple_of(owner * shard + q * piece, piece), piece)]

    def weight_direct(offset, q):
        return remote(weight_ref.at[pl.ds(q * piece, piece)], weight_rows(me, q),
                      w_send.at[offset - 1, q], w_recv.at[offset - 1, q], dp=peer(offset))

    def weight_side(offset, q):
        if offset == 0:
            src = weight_ref.at[pl.ds(q * piece, piece)]
        else:
            src = weight_rows(source(offset) + core, q)
        return remote(src, weight_rows(source(offset) + core, q),
                      w_side_send.at[offset, q], w_side_recv.at[offset, q], dp=sibling)

    for q in range(CHUNKS):
        for offset in range(1, chips):
            weight_direct(offset, q).start()
        weight_side(0, q).start()
    epoch_load.start()
    for q in range(CHUNKS):
        for offset in range(1, chips):
            weight_direct(offset, q).wait_recv()
            weight_side(offset, q).start()
    shard_load.wait()
    for q in range(CHUNKS):
        for offset in range(chips):
            weight_side(offset, q).wait_recv()

    @pl.when(s == 0)
    def _():
        stream_load.wait()

    @pl.when(s == last)
    def _():
        top_load.wait()

    epoch_load.wait()

    def columns(p):
        return slice(p * span, (p + 1) * span)

    def send_rows(m, p):
        return remote(decoded_ref.at[block(m), columns(p)], rows_in.at[block(m), columns(p)],
                      x_send.at[m, p], x_recv.at[m, p], section=after)

    def send_cot(m, p):
        return remote(cot_out.at[block(m), columns(p)], cot_in.at[block(m), columns(p)],
                      g_send.at[m, p], g_recv.at[m, p], section=before)

    def send_normed(offset):
        other = lax.rem(me + offset, replicas)
        return remote(normed.at[:, pl.ds(pl.multiple_of(other * shard, shard), shard)],
                      normed_all.at[pl.ds(pl.multiple_of(me * total, total), total)],
                      n_send.at[offset - 1], n_recv.at[offset - 1], dp=other)

    own_normed = pltpu.make_async_copy(
        normed.at[:, pl.ds(pl.multiple_of(me * shard, shard), shard)],
        normed_all.at[pl.ds(pl.multiple_of(me * total, total), total)], load_sem.at[3])

    def cot_rows(owner, m):
        return cot_all.at[pl.ds(pl.multiple_of(owner * total + m * step_rows, step_rows), step_rows)]

    def cot_direct(offset, m):
        return remote(cot_in.at[block(m)], cot_rows(me, m),
                      c_send.at[offset - 1, m], c_recv.at[offset - 1, m], dp=peer(offset))

    def cot_side(offset, m):
        owner = source(offset) + core
        src = cot_in.at[block(m)] if offset == 0 else cot_rows(owner, m)
        return remote(src, cot_rows(owner, m),
                      c_side_send.at[offset, m], c_side_recv.at[offset, m], dp=sibling)

    def cot_own(m):
        return pltpu.make_async_copy(cot_in.at[block(m)], cot_rows(me, m), own_sem.at[m])

    def relay(m):
        for offset in range(1, chips):
            cot_direct(offset, m).wait_recv()
            cot_side(offset, m).start()

    def squared(m):
        total_squares = jnp.zeros((step_rows, 1), jnp.float32)
        for p in range(PIECES):
            part = rows_in[block(m), columns(p)].astype(jnp.float32)
            total_squares += jnp.sum(part * part, axis=-1, keepdims=True)
        return lax.rsqrt(total_squares / width + epsilon)

    def forward(m):
        for p in range(PIECES):
            @pl.when(s > 0)
            def _():
                send_rows(m, p).wait_recv()

            piece_rows = rows_in[block(m), columns(p)]
            for start in range(0, width, TILE):
                part = jnp.dot(piece_rows, weight[columns(p), start:start + TILE],
                               preferred_element_type=jnp.float32)
                if p > 0:
                    part += product[block(m), start:start + TILE]
                product[block(m), start:start + TILE] = part
        scale = squared(m)
        squares = jnp.zeros((step_rows, 1), jnp.float32)
        for p in range(PIECES):
            values = rows_in[block(m), columns(p)].astype(jnp.float32)
            part = values + scale * product[block(m), columns(p)]
            product[block(m), columns(p)] = part
            squares += jnp.sum(part * part, axis=-1, keepdims=True)
        bound = 2.0 * jnp.sqrt(squares / width + epsilon)
        entry = ids_ref[0, m]
        for p in range(PIECES):
            base = epoch[entry, :, columns(p)].astype(jnp.float32)
            delta = jnp.clip(product[block(m), columns(p)] - base, -bound, bound).astype(jnp.bfloat16)
            decoded_ref[block(m), columns(p)] = (
                base + delta.astype(jnp.float32)).astype(jnp.bfloat16)

            @pl.when(s < last)
            def _():
                send_rows(m, p).start()

        for p in range(PIECES):
            values = rows_in[block(m), columns(p)].astype(jnp.float32)
            normed[block(m), columns(p)] = (values * scale).astype(jnp.bfloat16)

    def back_product(m, wait):
        for p in range(PIECES):
            if wait:
                send_cot(m, p).wait_recv()
            incoming = cot_in[block(m), columns(p)]
            for start in range(0, width, TILE):
                part = lax.dot_general(incoming, weight[start:start + TILE, columns(p)],
                                       (((1,), (1,)), ((), ())), preferred_element_type=jnp.float32)
                if p > 0:
                    part += ahead[block(m), start:start + TILE]
                ahead[block(m), start:start + TILE] = part

    def backward(m):
        @pl.when((s < last) & (s > 0))
        def _():
            back_product(m, True)

        @pl.when(s == 0)
        def _():
            for p in range(PIECES):
                send_cot(m, p).wait_recv()

        @pl.when(s > 0)
        def _():
            scale = squared(m)
            along = jnp.zeros((step_rows, 1), jnp.float32)
            for p in range(PIECES):
                along += jnp.sum(
                    ahead[block(m), columns(p)] * rows_in[block(m), columns(p)].astype(jnp.float32),
                    axis=-1, keepdims=True)
            pull = scale * scale * (along / width)
            for p in range(PIECES):
                values = rows_in[block(m), columns(p)].astype(jnp.float32)
                through = scale * (ahead[block(m), columns(p)] - values * pull)
                cot_out[block(m), columns(p)] = (
                    cot_in[block(m), columns(p)].astype(jnp.float32) + through).astype(jnp.bfloat16)
                send_cot(m, p).start()

        cot_side(0, m).start()
        for offset in range(1, chips):
            cot_direct(offset, m).start()
        cot_own(m).start()

        @pl.when(m > 0)
        def _():
            relay(m - 1)

    @pl.when(s == last)
    def _():
        lax.fori_loop(0, blocks, lambda m, carry: (back_product(m, False), carry)[1], 0)

    lag = jnp.minimum(blocks, (last - s) * 3)

    def step(k, carry):
        @pl.when(k < blocks)
        def _():
            forward(k)

        @pl.when(k == blocks - 1)
        def _():
            own_normed.start()
            for offset in range(1, replicas):
                send_normed(offset).start()

        @pl.when((k >= lag) & (k < lag + blocks))
        def _():
            backward(k - lag)

        return carry

    lax.fori_loop(0, 2 * blocks, step, 0)
    relay(blocks - 1)

    own_normed.wait()
    for offset in range(1, replicas):
        send_normed(offset).wait_send()
        send_normed(offset).wait_recv()
    for q in range(CHUNKS):
        for offset in range(1, chips):
            weight_direct(offset, q).wait_send()
        for offset in range(chips):
            weight_side(offset, q).wait_send()

    def finish(m, carry):
        @pl.when(s < last)
        def _():
            for p in range(PIECES):
                send_rows(m, p).wait_send()

        @pl.when(s > 0)
        def _():
            for p in range(PIECES):
                send_cot(m, p).wait_send()

        cot_own(m).wait()
        for offset in range(1, chips):
            cot_direct(offset, m).wait_send()
        for offset in range(chips):
            cot_side(offset, m).wait_send()
            cot_side(offset, m).wait_recv()
        return carry

    lax.fori_loop(0, blocks, finish, 0)


def local(sections, replicas, stream_in, sample_ids, epoch_buffer, layer_weight, top_cotangent):
    total, width = stream_in.shape
    blocks = sample_ids.shape[1]
    shard = layer_weight.shape[1]
    chips = replicas // 2
    dma = pltpu.SemaphoreType.DMA
    vmem = pl.BlockSpec(memory_space=pltpu.VMEM)
    anywhere = pl.BlockSpec(memory_space=pl.ANY)
    far = max(chips - 1, 1)
    decoded, normed_all, cot_all = pl.pallas_call(
        functools.partial(relay_kernel, sections, replicas, blocks),
        out_shape=(
            jax.ShapeDtypeStruct((total, width), jnp.bfloat16),
            jax.ShapeDtypeStruct((replicas * total, shard), jnp.bfloat16),
            jax.ShapeDtypeStruct((replicas * total, width), jnp.bfloat16),
        ),
        in_specs=[pl.BlockSpec(memory_space=pltpu.SMEM)] + [anywhere] * 4,
        out_specs=(vmem, anywhere, anywhere),
        scratch_shapes=[
            pltpu.VMEM((width, width), jnp.bfloat16),
            pltpu.VMEM((total, width), jnp.bfloat16),
            pltpu.VMEM((total, width), jnp.bfloat16),
            pltpu.VMEM((total, width), jnp.bfloat16),
            pltpu.VMEM((total, width), jnp.bfloat16),
            pltpu.VMEM((total, width), jnp.float32),
            pltpu.VMEM((total, width), jnp.float32),
            pltpu.VMEM(epoch_buffer.shape[1:], jnp.bfloat16),
            dma((5,)),
            dma((far, CHUNKS)), dma((far, CHUNKS)), dma((chips, CHUNKS)), dma((chips, CHUNKS)),
            dma((blocks, PIECES)), dma((blocks, PIECES)), dma((blocks, PIECES)), dma((blocks, PIECES)),
            dma((replicas - 1,)), dma((replicas - 1,)),
            dma((far, blocks)), dma((far, blocks)), dma((chips, blocks)), dma((chips, blocks)),
            dma((blocks,)),
        ],
        compiler_params=pltpu.CompilerParams(
            collective_id=0, has_side_effects=True, vmem_limit_bytes=60 * 1024 * 1024),
    )(sample_ids, epoch_buffer, stream_in, layer_weight, top_cotangent)
    gradient = lax.dot_general(
        normed_all, cot_all, (((0,), (0,)), ((), ())), preferred_element_type=jnp.float32)
    return (decoded[None], gradient[None])


def solution(mesh):
    in_specs = (
        P("dp", None),
        P("dp", None),
        P("section", "dp", None, None),
        P("section", "dp", None),
        P("dp", None),
    )
    out_specs = (P("section", "dp", None), P("section", "dp", None))
    body = functools.partial(local, mesh.shape["section"], mesh.shape["dp"])
    return jax.shard_map(body, mesh=mesh, in_specs=in_specs, out_specs=out_specs, check_vma=False)
```

```python
import functools

import jax
import jax.numpy as jnp
from jax import lax
from jax.experimental import pallas as pl
from jax.experimental.pallas import tpu as pltpu
from jax.sharding import PartitionSpec as P

epsilon = 1e-05
TILE = 512
PIECES = 4


def relay_kernel(sections, replicas, blocks, ids_ref, epoch_ref, stream_ref, weight_whole, top_ref,
                 decoded_ref, normed_all, cot_all,
                 weight, rows_in, normed, cot_in, cot_out, product, ahead, turned, partial, epoch,
                 load_sem, w_send, w_recv, w_side_send, w_side_recv,
                 x_send, x_recv, g_send, g_recv, n_send, n_recv,
                 c_send, c_recv, c_side_send, c_side_recv, own_sem):
    s = lax.axis_index("section")
    me = lax.axis_index("dp")
    last = sections - 1
    chips = replicas // 2
    chip, core = me // 2, lax.rem(me, 2)
    sibling = chip * 2 + 1 - core
    total, width = rows_in.shape
    step_rows = total // blocks
    weight_ref = weight_whole.at[0]
    shard = weight_ref.shape[0]
    span = width // PIECES
    chunks = w_send.shape[1]
    piece = shard // chunks
    after, before = lax.rem(s + 1, sections), lax.rem(s + last, sections)

    def peer(offset):
        return lax.rem(chip + offset, chips) * 2 + core

    def source(offset):
        return lax.rem(chip + chips - offset, chips) * 2

    def block(m):
        return pl.ds(pl.multiple_of(m * step_rows, step_rows), step_rows)

    def remote(src, dst, send, recv, **where):
        return pltpu.make_async_remote_copy(
            src_ref=src, dst_ref=dst, send_sem=send, recv_sem=recv,
            device_id=where, device_id_type=pl.DeviceIdType.MESH)

    barrier = pltpu.get_barrier_semaphore()

    def greet(**where):
        pl.semaphore_signal(barrier, inc=1, device_id=where, device_id_type=pl.DeviceIdType.MESH)

    for offset in range(1, replicas):
        greet(dp=lax.rem(me + offset, replicas))

    @pl.when(s < last)
    def _():
        greet(section=after)

    @pl.when(s > 0)
    def _():
        greet(section=before)

    stream_load = pltpu.make_async_copy(stream_ref, rows_in, load_sem.at[0])
    top_load = pltpu.make_async_copy(top_ref, cot_in, load_sem.at[1])
    shard_load = pltpu.make_async_copy(
        weight_ref, weight.at[pl.ds(pl.multiple_of(me * shard, shard), shard)], load_sem.at[2])
    shard_load.start()
    epoch_load = pltpu.make_async_copy(epoch_ref.at[0], epoch, load_sem.at[4])

    @pl.when(s == 0)
    def _():
        stream_load.start()

    @pl.when(s == last)
    def _():
        top_load.start()

    pl.semaphore_wait(
        barrier, replicas - 1 + jnp.minimum(s, 1) + jnp.minimum(last - s, 1))

    def weight_rows(owner, q):
        return weight.at[pl.ds(pl.multiple_of(owner * shard + q * piece, piece), piece)]

    def weight_direct(offset, q):
        return remote(weight_ref.at[pl.ds(q * piece, piece)], weight_rows(me, q),
                      w_send.at[offset - 1, q], w_recv.at[offset - 1, q], dp=peer(offset))

    def weight_side(offset, q):
        if offset == 0:
            src = weight_ref.at[pl.ds(q * piece, piece)]
        else:
            src = weight_rows(source(offset) + core, q)
        return remote(src, weight_rows(source(offset) + core, q),
                      w_side_send.at[offset, q], w_side_recv.at[offset, q], dp=sibling)

    for q in range(chunks):
        for offset in range(1, chips):
            weight_direct(offset, q).start()
        weight_side(0, q).start()
    epoch_load.start()
    def turn(owner, q):
        first = pl.multiple_of(owner * shard + q * piece, piece)

        def turn_columns(j, carry):
            across = pl.ds(pl.multiple_of(j * TILE, TILE), TILE)
            turned[across, pl.ds(first, piece)] = weight[pl.ds(first, piece), across].T
            return carry

        lax.fori_loop(0, width // TILE, turn_columns, 0)

    shard_load.wait()
    for q in range(chunks):
        turn(me, q)
    for q in range(chunks):
        weight_side(0, q).wait_recv()
        turn(sibling, q)
    for q in range(chunks):
        for offset in range(1, chips):
            weight_direct(offset, q).wait_recv()
            weight_side(offset, q).start()
            turn(source(offset) + core, q)
        for offset in range(1, chips):
            weight_side(offset, q).wait_recv()
            turn(source(offset) + 1 - core, q)

    @pl.when(s == 0)
    def _():
        stream_load.wait()

    @pl.when(s == last)
    def _():
        top_load.wait()

    epoch_load.wait()

    def columns(p):
        return slice(p * span, (p + 1) * span)

    def send_rows(m, p):
        return remote(decoded_ref.at[block(m), columns(p)], rows_in.at[block(m), columns(p)],
                      x_send.at[m, p], x_recv.at[m, p], section=after)

    def send_cot(m, p):
        return remote(cot_out.at[block(m), columns(p)], cot_in.at[block(m), columns(p)],
                      g_send.at[m, p], g_recv.at[m, p], section=before)

    def send_normed(offset):
        other = lax.rem(me + offset, replicas)
        return remote(normed.at[:, pl.ds(pl.multiple_of(other * shard, shard), shard)],
                      normed_all.at[pl.ds(pl.multiple_of(me * total, total), total)],
                      n_send.at[offset - 1], n_recv.at[offset - 1], dp=other)

    own_normed = pltpu.make_async_copy(
        normed.at[:, pl.ds(pl.multiple_of(me * shard, shard), shard)],
        normed_all.at[pl.ds(pl.multiple_of(me * total, total), total)], load_sem.at[3])

    def cot_rows(owner, m):
        return cot_all.at[pl.ds(pl.multiple_of(owner * total + m * step_rows, step_rows), step_rows)]

    def cot_direct(offset, m):
        return remote(cot_in.at[block(m)], cot_rows(me, m),
                      c_send.at[offset - 1, m], c_recv.at[offset - 1, m], dp=peer(offset))

    def cot_side(offset, m):
        owner = source(offset) + core
        src = cot_in.at[block(m)] if offset == 0 else cot_rows(owner, m)
        return remote(src, cot_rows(owner, m),
                      c_side_send.at[offset, m], c_side_recv.at[offset, m], dp=sibling)

    def cot_own(m):
        return pltpu.make_async_copy(cot_in.at[block(m)], cot_rows(me, m), own_sem.at[m])

    def relay(m):
        for offset in range(1, chips):
            cot_direct(offset, m).wait_recv()
            cot_side(offset, m).start()

    def squared(m):
        total_squares = jnp.zeros((step_rows, 1), jnp.float32)
        for p in range(PIECES):
            part = rows_in[block(m), columns(p)].astype(jnp.float32)
            total_squares += jnp.sum(part * part, axis=-1, keepdims=True)
        return lax.rsqrt(total_squares / width + epsilon)

    def multiply(matrix, rows, result, m, p):
        held = rows[block(m), columns(p)]
        for start in range(0, width, TILE):
            part = lax.dot_general(matrix[start:start + TILE, columns(p)], held,
                                   (((1,), (1,)), ((), ())), preferred_element_type=jnp.float32)
            if p > 0:
                part += partial[start:start + TILE, :]
            if p < PIECES - 1:
                partial[start:start + TILE, :] = part
            else:
                result[block(m), start:start + TILE] = part.T

    def forward(m):
        for p in range(PIECES):
            @pl.when(s > 0)
            def _():
                send_rows(m, p).wait_recv()

            multiply(turned, rows_in, product, m, p)
        scale = squared(m)
        squares = jnp.zeros((step_rows, 1), jnp.float32)
        for p in range(PIECES):
            values = rows_in[block(m), columns(p)].astype(jnp.float32)
            part = values + scale * product[block(m), columns(p)]
            product[block(m), columns(p)] = part
            squares += jnp.sum(part * part, axis=-1, keepdims=True)
        bound = 2.0 * jnp.sqrt(squares / width + epsilon)
        entry = ids_ref[0, m]
        for p in range(PIECES):
            base = epoch[entry, :, columns(p)].astype(jnp.float32)
            delta = jnp.clip(product[block(m), columns(p)] - base, -bound, bound).astype(jnp.bfloat16)
            decoded_ref[block(m), columns(p)] = (
                base + delta.astype(jnp.float32)).astype(jnp.bfloat16)

            @pl.when(s < last)
            def _():
                send_rows(m, p).start()

        for p in range(PIECES):
            values = rows_in[block(m), columns(p)].astype(jnp.float32)
            normed[block(m), columns(p)] = (values * scale).astype(jnp.bfloat16)

    def back_product(m, wait):
        for p in range(PIECES):
            if wait:
                send_cot(m, p).wait_recv()
            multiply(weight, cot_in, ahead, m, p)

    def backward(m):
        @pl.when((s < last) & (s > 0))
        def _():
            back_product(m, True)

        @pl.when(s == 0)
        def _():
            for p in range(PIECES):
                send_cot(m, p).wait_recv()

        @pl.when(s > 0)
        def _():
            scale = squared(m)
            along = jnp.zeros((step_rows, 1), jnp.float32)
            for p in range(PIECES):
                along += jnp.sum(
                    ahead[block(m), columns(p)] * rows_in[block(m), columns(p)].astype(jnp.float32),
                    axis=-1, keepdims=True)
            pull = scale * scale * (along / width)
            for p in range(PIECES):
                values = rows_in[block(m), columns(p)].astype(jnp.float32)
                through = scale * (ahead[block(m), columns(p)] - values * pull)
                cot_out[block(m), columns(p)] = (
                    cot_in[block(m), columns(p)].astype(jnp.float32) + through).astype(jnp.bfloat16)
                send_cot(m, p).start()

        cot_side(0, m).start()
        for offset in range(1, chips):
            cot_direct(offset, m).start()
        cot_own(m).start()

        @pl.when(m > 0)
        def _():
            relay(m - 1)

    @pl.when(s == last)
    def _():
        lax.fori_loop(0, blocks, lambda m, carry: (back_product(m, False), carry)[1], 0)

    lag = jnp.minimum(blocks, (last - s) * 3)

    def step(k, carry):
        @pl.when(k < blocks)
        def _():
            forward(k)

        @pl.when(k == blocks - 1)
        def _():
            own_normed.start()
            for offset in range(1, replicas):
                send_normed(offset).start()

        @pl.when((k >= lag) & (k < lag + blocks))
        def _():
            backward(k - lag)

        return carry

    lax.fori_loop(0, 2 * blocks, step, 0)
    relay(blocks - 1)

    own_normed.wait()
    for offset in range(1, replicas):
        send_normed(offset).wait_send()
        send_normed(offset).wait_recv()
    for q in range(chunks):
        for offset in range(1, chips):
            weight_direct(offset, q).wait_send()
        for offset in range(chips):
            weight_side(offset, q).wait_send()

    def finish(m, carry):
        @pl.when(s < last)
        def _():
            for p in range(PIECES):
                send_rows(m, p).wait_send()

        @pl.when(s > 0)
        def _():
            for p in range(PIECES):
                send_cot(m, p).wait_send()

        cot_own(m).wait()
        for offset in range(1, chips):
            cot_direct(offset, m).wait_send()
        for offset in range(chips):
            cot_side(offset, m).wait_send()
            cot_side(offset, m).wait_recv()
        return carry

    lax.fori_loop(0, blocks, finish, 0)


def local(sections, replicas, stream_in, sample_ids, epoch_buffer, layer_weight, top_cotangent):
    total, width = stream_in.shape
    blocks = sample_ids.shape[1]
    shard = layer_weight.shape[1]
    chunks = max(1, min(4, shard // 128))
    chips = replicas // 2
    dma = pltpu.SemaphoreType.DMA
    vmem = pl.BlockSpec(memory_space=pltpu.VMEM)
    anywhere = pl.BlockSpec(memory_space=pl.ANY)
    far = max(chips - 1, 1)
    decoded, normed_all, cot_all = pl.pallas_call(
        functools.partial(relay_kernel, sections, replicas, blocks),
        out_shape=(
            jax.ShapeDtypeStruct((total, width), jnp.bfloat16),
            jax.ShapeDtypeStruct((replicas * total, shard), jnp.bfloat16),
            jax.ShapeDtypeStruct((replicas * total, width), jnp.bfloat16),
        ),
        in_specs=[pl.BlockSpec(memory_space=pltpu.SMEM)] + [anywhere] * 4,
        out_specs=(vmem, anywhere, anywhere),
        scratch_shapes=[
            pltpu.VMEM((width, width), jnp.bfloat16),
            pltpu.VMEM((total, width), jnp.bfloat16),
            pltpu.VMEM((total, width), jnp.bfloat16),
            pltpu.VMEM((total, width), jnp.bfloat16),
            pltpu.VMEM((total, width), jnp.bfloat16),
            pltpu.VMEM((total, width), jnp.float32),
            pltpu.VMEM((total, width), jnp.float32),
            pltpu.VMEM((width, width), jnp.bfloat16),
            pltpu.VMEM((width, total // blocks), jnp.float32),
            pltpu.VMEM(epoch_buffer.shape[1:], jnp.bfloat16),
            dma((5,)),
            dma((far, chunks)), dma((far, chunks)), dma((chips, chunks)), dma((chips, chunks)),
            dma((blocks, PIECES)), dma((blocks, PIECES)), dma((blocks, PIECES)), dma((blocks, PIECES)),
            dma((replicas - 1,)), dma((replicas - 1,)),
            dma((far, blocks)), dma((far, blocks)), dma((chips, blocks)), dma((chips, blocks)),
            dma((blocks,)),
        ],
        compiler_params=pltpu.CompilerParams(
            collective_id=0, has_side_effects=True, vmem_limit_bytes=60 * 1024 * 1024),
    )(sample_ids, epoch_buffer, stream_in, layer_weight, top_cotangent)
    gradient = lax.dot_general(
        normed_all, cot_all, (((0,), (0,)), ((), ())), preferred_element_type=jnp.float32)
    return (decoded[None], gradient[None])


def solution(mesh):
    in_specs = (
        P("dp", None),
        P("dp", None),
        P("section", "dp", None, None),
        P("section", "dp", None),
        P("dp", None),
    )
    out_specs = (P("section", "dp", None), P("section", "dp", None))
    body = functools.partial(local, mesh.shape["section"], mesh.shape["dp"])
    return jax.shard_map(body, mesh=mesh, in_specs=in_specs, out_specs=out_specs, check_vma=False)
```

```python
import functools

import jax
import jax.numpy as jnp
from jax import lax
from jax.experimental import pallas as pl
from jax.experimental.pallas import tpu as pltpu
from jax.sharding import PartitionSpec as P

epsilon = 1e-05
TILE = 512
PIECES = 4


def relay_kernel(sections, replicas, blocks, ids_ref, epoch_ref, stream_ref, weight_whole, top_ref,
                 decoded_ref, normed_all, cot_all,
                 weight, rows_in, normed, cot_in, cot_out, product, ahead, epoch,
                 load_sem, w_send, w_recv, w_side_send, w_side_recv,
                 x_send, x_recv, g_send, g_recv, n_send, n_recv,
                 c_send, c_recv, c_side_send, c_side_recv, own_sem):
    s = lax.axis_index("section")
    me = lax.axis_index("dp")
    last = sections - 1
    chips = replicas // 2
    chip, core = me // 2, lax.rem(me, 2)
    sibling = chip * 2 + 1 - core
    total, width = rows_in.shape
    step_rows = total // blocks
    weight_ref = weight_whole.at[0]
    shard = weight_ref.shape[0]
    span = width // PIECES
    chunks = w_send.shape[1]
    piece = shard // chunks
    after, before = lax.rem(s + 1, sections), lax.rem(s + last, sections)

    def peer(offset):
        return lax.rem(chip + offset, chips) * 2 + core

    def source(offset):
        return lax.rem(chip + chips - offset, chips) * 2

    def block(m):
        return pl.ds(pl.multiple_of(m * step_rows, step_rows), step_rows)

    def remote(src, dst, send, recv, **where):
        return pltpu.make_async_remote_copy(
            src_ref=src, dst_ref=dst, send_sem=send, recv_sem=recv,
            device_id=where, device_id_type=pl.DeviceIdType.MESH)

    barrier = pltpu.get_barrier_semaphore()

    def greet(**where):
        pl.semaphore_signal(barrier, inc=1, device_id=where, device_id_type=pl.DeviceIdType.MESH)

    for offset in range(1, replicas):
        greet(dp=lax.rem(me + offset, replicas))

    @pl.when(s < last)
    def _():
        greet(section=after)

    @pl.when(s > 0)
    def _():
        greet(section=before)

    stream_load = pltpu.make_async_copy(stream_ref, rows_in, load_sem.at[0])
    top_load = pltpu.make_async_copy(top_ref, cot_in, load_sem.at[1])
    shard_load = pltpu.make_async_copy(
        weight_ref, weight.at[pl.ds(pl.multiple_of(me * shard, shard), shard)], load_sem.at[2])
    shard_load.start()
    epoch_load = pltpu.make_async_copy(epoch_ref.at[0], epoch, load_sem.at[4])

    @pl.when(s == 0)
    def _():
        stream_load.start()

    @pl.when(s == last)
    def _():
        top_load.start()

    pl.semaphore_wait(
        barrier, replicas - 1 + jnp.minimum(s, 1) + jnp.minimum(last - s, 1))

    def weight_rows(owner, q):
        return weight.at[pl.ds(pl.multiple_of(owner * shard + q * piece, piece), piece)]

    def weight_direct(offset, q):
        return remote(weight_ref.at[pl.ds(q * piece, piece)], weight_rows(me, q),
                      w_send.at[offset - 1, q], w_recv.at[offset - 1, q], dp=peer(offset))

    def weight_side(offset, q):
        if offset == 0:
            src = weight_ref.at[pl.ds(q * piece, piece)]
        else:
            src = weight_rows(source(offset) + core, q)
        return remote(src, weight_rows(source(offset) + core, q),
                      w_side_send.at[offset, q], w_side_recv.at[offset, q], dp=sibling)

    for q in range(chunks):
        for offset in range(1, chips):
            weight_direct(offset, q).start()
        weight_side(0, q).start()
    epoch_load.start()
    def absorb(first, depth):
        @pl.when(s == 0)
        def _():
            lanes = pl.ds(pl.multiple_of(first, depth), depth)
            for start in range(0, width, TILE):
                product[:, start:start + TILE] += jnp.dot(
                    rows_in[:, lanes], weight[lanes, start:start + TILE],
                    preferred_element_type=jnp.float32)

    @pl.when(s == 0)
    def _():
        stream_load.wait()
        product[...] = jnp.zeros_like(product)

    shard_load.wait()
    absorb(me * shard, shard)
    for q in range(chunks):
        weight_side(0, q).wait_recv()
    absorb(sibling * shard, shard)
    for q in range(chunks):
        for offset in range(1, chips):
            weight_direct(offset, q).wait_recv()
            weight_side(offset, q).start()
        for offset in range(1, chips):
            absorb((source(offset) + core) * shard + q * piece, piece)
        for offset in range(1, chips):
            weight_side(offset, q).wait_recv()
            absorb((source(offset) + 1 - core) * shard + q * piece, piece)

    @pl.when(s == last)
    def _():
        top_load.wait()

    epoch_load.wait()

    def columns(p):
        return slice(p * span, (p + 1) * span)

    def send_rows(m, p):
        return remote(decoded_ref.at[block(m), columns(p)], rows_in.at[block(m), columns(p)],
                      x_send.at[m, p], x_recv.at[m, p], section=after)

    def send_cot(m, p):
        return remote(cot_out.at[block(m), columns(p)], cot_in.at[block(m), columns(p)],
                      g_send.at[m, p], g_recv.at[m, p], section=before)

    def send_normed(offset):
        other = lax.rem(me + offset, replicas)
        return remote(normed.at[:, pl.ds(pl.multiple_of(other * shard, shard), shard)],
                      normed_all.at[pl.ds(pl.multiple_of(me * total, total), total)],
                      n_send.at[offset - 1], n_recv.at[offset - 1], dp=other)

    own_normed = pltpu.make_async_copy(
        normed.at[:, pl.ds(pl.multiple_of(me * shard, shard), shard)],
        normed_all.at[pl.ds(pl.multiple_of(me * total, total), total)], load_sem.at[3])

    def cot_rows(owner, m):
        return cot_all.at[pl.ds(pl.multiple_of(owner * total + m * step_rows, step_rows), step_rows)]

    def cot_direct(offset, m):
        return remote(cot_in.at[block(m)], cot_rows(me, m),
                      c_send.at[offset - 1, m], c_recv.at[offset - 1, m], dp=peer(offset))

    def cot_side(offset, m):
        owner = source(offset) + core
        src = cot_in.at[block(m)] if offset == 0 else cot_rows(owner, m)
        return remote(src, cot_rows(owner, m),
                      c_side_send.at[offset, m], c_side_recv.at[offset, m], dp=sibling)

    def cot_own(m):
        return pltpu.make_async_copy(cot_in.at[block(m)], cot_rows(me, m), own_sem.at[m])

    def relay(m):
        for offset in range(1, chips):
            cot_direct(offset, m).wait_recv()
            cot_side(offset, m).start()

    def squared(m):
        total_squares = jnp.zeros((step_rows, 1), jnp.float32)
        for p in range(PIECES):
            part = rows_in[block(m), columns(p)].astype(jnp.float32)
            total_squares += jnp.sum(part * part, axis=-1, keepdims=True)
        return lax.rsqrt(total_squares / width + epsilon)

    def forward(m):
        @pl.when(s > 0)
        def _():
            for p in range(PIECES):
                send_rows(m, p).wait_recv()
                piece_rows = rows_in[block(m), columns(p)]
                for start in range(0, width, TILE):
                    part = jnp.dot(piece_rows, weight[columns(p), start:start + TILE],
                                   preferred_element_type=jnp.float32)
                    if p > 0:
                        part += product[block(m), start:start + TILE]
                    product[block(m), start:start + TILE] = part

        scale = squared(m)
        squares = jnp.zeros((step_rows, 1), jnp.float32)
        for p in range(PIECES):
            values = rows_in[block(m), columns(p)].astype(jnp.float32)
            part = values + scale * product[block(m), columns(p)]
            product[block(m), columns(p)] = part
            squares += jnp.sum(part * part, axis=-1, keepdims=True)
        bound = 2.0 * jnp.sqrt(squares / width + epsilon)
        entry = ids_ref[0, m]
        for p in range(PIECES):
            base = epoch[entry, :, columns(p)].astype(jnp.float32)
            delta = jnp.clip(product[block(m), columns(p)] - base, -bound, bound).astype(jnp.bfloat16)
            decoded_ref[block(m), columns(p)] = (
                base + delta.astype(jnp.float32)).astype(jnp.bfloat16)

            @pl.when(s < last)
            def _():
                send_rows(m, p).start()

        for p in range(PIECES):
            values = rows_in[block(m), columns(p)].astype(jnp.float32)
            normed[block(m), columns(p)] = (values * scale).astype(jnp.bfloat16)

    def back_product(m, wait):
        for p in range(PIECES):
            if wait:
                send_cot(m, p).wait_recv()
            incoming = cot_in[block(m), columns(p)]
            for start in range(0, width, TILE):
                part = lax.dot_general(incoming, weight[start:start + TILE, columns(p)],
                                       (((1,), (1,)), ((), ())), preferred_element_type=jnp.float32)
                if p > 0:
                    part += ahead[block(m), start:start + TILE]
                ahead[block(m), start:start + TILE] = part

    def backward(m):
        @pl.when((s < last) & (s > 0))
        def _():
            back_product(m, True)

        @pl.when(s == 0)
        def _():
            for p in range(PIECES):
                send_cot(m, p).wait_recv()

        @pl.when(s > 0)
        def _():
            scale = squared(m)
            along = jnp.zeros((step_rows, 1), jnp.float32)
            for p in range(PIECES):
                along += jnp.sum(
                    ahead[block(m), columns(p)] * rows_in[block(m), columns(p)].astype(jnp.float32),
                    axis=-1, keepdims=True)
            pull = scale * scale * (along / width)
            for p in range(PIECES):
                values = rows_in[block(m), columns(p)].astype(jnp.float32)
                through = scale * (ahead[block(m), columns(p)] - values * pull)
                cot_out[block(m), columns(p)] = (
                    cot_in[block(m), columns(p)].astype(jnp.float32) + through).astype(jnp.bfloat16)
                send_cot(m, p).start()

        cot_side(0, m).start()
        for offset in range(1, chips):
            cot_direct(offset, m).start()
        cot_own(m).start()

        @pl.when(m > 0)
        def _():
            relay(m - 1)

    @pl.when(s == last)
    def _():
        lax.fori_loop(0, blocks, lambda m, carry: (back_product(m, False), carry)[1], 0)

    lag = jnp.minimum(blocks, (last - s) * 3)

    def step(k, carry):
        @pl.when(k < blocks)
        def _():
            forward(k)

        @pl.when(k == blocks - 1)
        def _():
            own_normed.start()
            for offset in range(1, replicas):
                send_normed(offset).start()

        @pl.when((k >= lag) & (k < lag + blocks))
        def _():
            backward(k - lag)

        return carry

    lax.fori_loop(0, 2 * blocks, step, 0)
    relay(blocks - 1)

    own_normed.wait()
    for offset in range(1, replicas):
        send_normed(offset).wait_send()
        send_normed(offset).wait_recv()
    for q in range(chunks):
        for offset in range(1, chips):
            weight_direct(offset, q).wait_send()
        for offset in range(chips):
            weight_side(offset, q).wait_send()

    def finish(m, carry):
        @pl.when(s < last)
        def _():
            for p in range(PIECES):
                send_rows(m, p).wait_send()

        @pl.when(s > 0)
        def _():
            for p in range(PIECES):
                send_cot(m, p).wait_send()

        cot_own(m).wait()
        for offset in range(1, chips):
            cot_direct(offset, m).wait_send()
        for offset in range(chips):
            cot_side(offset, m).wait_send()
            cot_side(offset, m).wait_recv()
        return carry

    lax.fori_loop(0, blocks, finish, 0)


def gradient_kernel(normed_ref, cot_ref, gradient_ref, flipped):
    @pl.when(pl.program_id(0) == 0)
    def _():
        flipped[...] = normed_ref[...].T

    gradient_ref[...] = jnp.dot(flipped[...], cot_ref[...], preferred_element_type=jnp.float32)


def local(sections, replicas, stream_in, sample_ids, epoch_buffer, layer_weight, top_cotangent):
    total, width = stream_in.shape
    blocks = sample_ids.shape[1]
    shard = layer_weight.shape[1]
    chunks = max(1, min(4, shard // 128))
    chips = replicas // 2
    dma = pltpu.SemaphoreType.DMA
    vmem = pl.BlockSpec(memory_space=pltpu.VMEM)
    anywhere = pl.BlockSpec(memory_space=pl.ANY)
    far = max(chips - 1, 1)
    decoded, normed_all, cot_all = pl.pallas_call(
        functools.partial(relay_kernel, sections, replicas, blocks),
        out_shape=(
            jax.ShapeDtypeStruct((total, width), jnp.bfloat16),
            jax.ShapeDtypeStruct((replicas * total, shard), jnp.bfloat16),
            jax.ShapeDtypeStruct((replicas * total, width), jnp.bfloat16),
        ),
        in_specs=[pl.BlockSpec(memory_space=pltpu.SMEM)] + [anywhere] * 4,
        out_specs=(vmem, anywhere, anywhere),
        scratch_shapes=[
            pltpu.VMEM((width, width), jnp.bfloat16),
            pltpu.VMEM((total, width), jnp.bfloat16),
            pltpu.VMEM((total, width), jnp.bfloat16),
            pltpu.VMEM((total, width), jnp.bfloat16),
            pltpu.VMEM((total, width), jnp.bfloat16),
            pltpu.VMEM((total, width), jnp.float32),
            pltpu.VMEM((total, width), jnp.float32),
            pltpu.VMEM(epoch_buffer.shape[1:], jnp.bfloat16),
            dma((5,)),
            dma((far, chunks)), dma((far, chunks)), dma((chips, chunks)), dma((chips, chunks)),
            dma((blocks, PIECES)), dma((blocks, PIECES)), dma((blocks, PIECES)), dma((blocks, PIECES)),
            dma((replicas - 1,)), dma((replicas - 1,)),
            dma((far, blocks)), dma((far, blocks)), dma((chips, blocks)), dma((chips, blocks)),
            dma((blocks,)),
        ],
        compiler_params=pltpu.CompilerParams(
            collective_id=0, has_side_effects=True, vmem_limit_bytes=60 * 1024 * 1024),
    )(sample_ids, epoch_buffer, stream_in, layer_weight, top_cotangent)
    gradient = pl.pallas_call(
        gradient_kernel,
        grid=(width // TILE,),
        out_shape=jax.ShapeDtypeStruct((shard, width), jnp.float32),
        in_specs=[
            pl.BlockSpec((replicas * total, shard), lambda j: (0, 0)),
            pl.BlockSpec((replicas * total, TILE), lambda j: (0, j)),
        ],
        out_specs=pl.BlockSpec((shard, TILE), lambda j: (0, j)),
        scratch_shapes=[pltpu.VMEM((shard, replicas * total), jnp.bfloat16)],
        compiler_params=pltpu.CompilerParams(vmem_limit_bytes=60 * 1024 * 1024),
    )(normed_all, cot_all)
    return (decoded[None], gradient[None])


def solution(mesh):
    in_specs = (
        P("dp", None),
        P("dp", None),
        P("section", "dp", None, None),
        P("section", "dp", None),
        P("dp", None),
    )
    out_specs = (P("section", "dp", None), P("section", "dp", None))
    body = functools.partial(local, mesh.shape["section"], mesh.shape["dp"])
    return jax.shard_map(body, mesh=mesh, in_specs=in_specs, out_specs=out_specs, check_vma=False)
```

```python
import functools

import jax
import jax.numpy as jnp
from jax import lax
from jax.experimental import pallas as pl
from jax.experimental.pallas import tpu as pltpu
from jax.sharding import PartitionSpec as P

epsilon = 1e-05
TILE = 512
PIECES = 4


def relay_kernel(sections, replicas, blocks, ids_ref, epoch_ref, stream_ref, weight_whole, top_ref,
                 decoded_ref, normed_all, cot_all,
                 weight, rows_in, normed, cot_in, cot_out, product, ahead, epoch,
                 load_sem, w_send, w_recv, w_side_send, w_side_recv,
                 x_send, x_recv, g_send, g_recv, n_send, n_recv,
                 c_send, c_recv, c_side_send, c_side_recv, own_sem):
    s = lax.axis_index("section")
    me = lax.axis_index("dp")
    last = sections - 1
    chips = replicas // 2
    chip, core = me // 2, lax.rem(me, 2)
    sibling = chip * 2 + 1 - core
    total, width = rows_in.shape
    step_rows = total // blocks
    weight_ref = weight_whole.at[0]
    shard = weight_ref.shape[0]
    span = width // PIECES
    chunks = w_send.shape[1]
    piece = shard // chunks
    after, before = lax.rem(s + 1, sections), lax.rem(s + last, sections)

    def peer(offset):
        return lax.rem(chip + offset, chips) * 2 + core

    def source(offset):
        return lax.rem(chip + chips - offset, chips) * 2

    def block(m):
        return pl.ds(pl.multiple_of(m * step_rows, step_rows), step_rows)

    def remote(src, dst, send, recv, **where):
        return pltpu.make_async_remote_copy(
            src_ref=src, dst_ref=dst, send_sem=send, recv_sem=recv,
            device_id=where, device_id_type=pl.DeviceIdType.MESH)

    barrier = pltpu.get_barrier_semaphore()

    def greet(**where):
        pl.semaphore_signal(barrier, inc=1, device_id=where, device_id_type=pl.DeviceIdType.MESH)

    for offset in range(1, replicas):
        greet(dp=lax.rem(me + offset, replicas))

    @pl.when(s < last)
    def _():
        greet(section=after)

    @pl.when(s > 0)
    def _():
        greet(section=before)

    stream_load = pltpu.make_async_copy(stream_ref, rows_in, load_sem.at[0])
    top_load = pltpu.make_async_copy(top_ref, cot_in, load_sem.at[1])
    shard_load = pltpu.make_async_copy(
        weight_ref, weight.at[pl.ds(pl.multiple_of(me * shard, shard), shard)], load_sem.at[2])
    shard_load.start()
    epoch_load = pltpu.make_async_copy(epoch_ref.at[0], epoch, load_sem.at[4])

    @pl.when(s == 0)
    def _():
        stream_load.start()

    @pl.when(s == last)
    def _():
        top_load.start()

    pl.semaphore_wait(
        barrier, replicas - 1 + jnp.minimum(s, 1) + jnp.minimum(last - s, 1))

    def weight_rows(owner, q):
        return weight.at[pl.ds(pl.multiple_of(owner * shard + q * piece, piece), piece)]

    def weight_direct(offset, q):
        return remote(weight_ref.at[pl.ds(q * piece, piece)], weight_rows(me, q),
                      w_send.at[offset - 1, q], w_recv.at[offset - 1, q], dp=peer(offset))

    def weight_side(offset, q):
        if offset == 0:
            src = weight_ref.at[pl.ds(q * piece, piece)]
        else:
            src = weight_rows(source(offset) + core, q)
        return remote(src, weight_rows(source(offset) + core, q),
                      w_side_send.at[offset, q], w_side_recv.at[offset, q], dp=sibling)

    for q in range(chunks):
        for offset in range(1, chips):
            weight_direct(offset, q).start()
        weight_side(0, q).start()
    epoch_load.start()
    def absorb(first, depth):
        @pl.when(s == 0)
        def _():
            lanes = pl.ds(pl.multiple_of(first, depth), depth)
            for start in range(0, width, TILE):
                product[:, start:start + TILE] += jnp.dot(
                    rows_in[:, lanes], weight[lanes, start:start + TILE],
                    preferred_element_type=jnp.float32)

    @pl.when(s == 0)
    def _():
        stream_load.wait()
        product[...] = jnp.zeros_like(product)

    shard_load.wait()
    absorb(me * shard, shard)
    for q in range(chunks):
        weight_side(0, q).wait_recv()
    absorb(sibling * shard, shard)
    for q in range(chunks):
        for offset in range(1, chips):
            weight_direct(offset, q).wait_recv()
            weight_side(offset, q).start()
        for offset in range(1, chips):
            absorb((source(offset) + core) * shard + q * piece, piece)
        for offset in range(1, chips):
            weight_side(offset, q).wait_recv()
            absorb((source(offset) + 1 - core) * shard + q * piece, piece)

    @pl.when(s == last)
    def _():
        top_load.wait()

    epoch_load.wait()

    def columns(p):
        return slice(p * span, (p + 1) * span)

    def send_rows(m, p):
        return remote(decoded_ref.at[block(m), columns(p)], rows_in.at[block(m), columns(p)],
                      x_send.at[m, p], x_recv.at[m, p], section=after)

    def send_cot(m, p):
        return remote(cot_out.at[block(m), columns(p)], cot_in.at[block(m), columns(p)],
                      g_send.at[m, p], g_recv.at[m, p], section=before)

    def send_normed(offset):
        other = lax.rem(me + offset, replicas)
        return remote(normed.at[:, pl.ds(pl.multiple_of(other * shard, shard), shard)],
                      normed_all.at[pl.ds(pl.multiple_of(me * total, total), total)],
                      n_send.at[offset - 1], n_recv.at[offset - 1], dp=other)

    own_normed = pltpu.make_async_copy(
        normed.at[:, pl.ds(pl.multiple_of(me * shard, shard), shard)],
        normed_all.at[pl.ds(pl.multiple_of(me * total, total), total)], load_sem.at[3])

    def cot_rows(owner, m):
        return cot_all.at[pl.ds(pl.multiple_of(owner * total + m * step_rows, step_rows), step_rows)]

    def cot_direct(offset, m):
        return remote(cot_in.at[block(m)], cot_rows(me, m),
                      c_send.at[offset - 1, m], c_recv.at[offset - 1, m], dp=peer(offset))

    def cot_side(offset, m):
        owner = source(offset) + core
        src = cot_in.at[block(m)] if offset == 0 else cot_rows(owner, m)
        return remote(src, cot_rows(owner, m),
                      c_side_send.at[offset, m], c_side_recv.at[offset, m], dp=sibling)

    def cot_own(m):
        return pltpu.make_async_copy(cot_in.at[block(m)], cot_rows(me, m), own_sem.at[m])

    def relay(m):
        for offset in range(1, chips):
            cot_direct(offset, m).wait_recv()
            cot_side(offset, m).start()

    def squared(m):
        total_squares = jnp.zeros((step_rows, 1), jnp.float32)
        for p in range(PIECES):
            part = rows_in[block(m), columns(p)].astype(jnp.float32)
            total_squares += jnp.sum(part * part, axis=-1, keepdims=True)
        return lax.rsqrt(total_squares / width + epsilon)

    def forward(m, count):
        group = pl.ds(pl.multiple_of(m * step_rows, step_rows), count * step_rows)

        @pl.when(s > 0)
        def _():
            for p in range(PIECES):
                for i in range(count):
                    send_rows(m + i, p).wait_recv()
                piece_rows = rows_in[group, columns(p)]
                for start in range(0, width, TILE):
                    part = jnp.dot(piece_rows, weight[columns(p), start:start + TILE],
                                   preferred_element_type=jnp.float32)
                    if p > 0:
                        part += product[group, start:start + TILE]
                    product[group, start:start + TILE] = part

        for i in range(count):
            scale = squared(m + i)
            squares = jnp.zeros((step_rows, 1), jnp.float32)
            for p in range(PIECES):
                values = rows_in[block(m + i), columns(p)].astype(jnp.float32)
                part = values + scale * product[block(m + i), columns(p)]
                product[block(m + i), columns(p)] = part
                squares += jnp.sum(part * part, axis=-1, keepdims=True)
            bound = 2.0 * jnp.sqrt(squares / width + epsilon)
            entry = ids_ref[0, m + i]
            for p in range(PIECES):
                base = epoch[entry, :, columns(p)].astype(jnp.float32)
                delta = jnp.clip(product[block(m + i), columns(p)] - base, -bound, bound).astype(
                    jnp.bfloat16)
                decoded_ref[block(m + i), columns(p)] = (
                    base + delta.astype(jnp.float32)).astype(jnp.bfloat16)

                @pl.when(s < last)
                def _():
                    send_rows(m + i, p).start()

            for p in range(PIECES):
                values = rows_in[block(m + i), columns(p)].astype(jnp.float32)
                normed[block(m + i), columns(p)] = (values * scale).astype(jnp.bfloat16)

    def back_product(m):
        for p in range(PIECES):
            send_cot(m, p).wait_recv()
            incoming = cot_in[block(m), columns(p)]
            for start in range(0, width, TILE):
                part = lax.dot_general(incoming, weight[start:start + TILE, columns(p)],
                                       (((1,), (1,)), ((), ())), preferred_element_type=jnp.float32)
                if p > 0:
                    part += ahead[block(m), start:start + TILE]
                ahead[block(m), start:start + TILE] = part

    def backward(m):
        @pl.when((s < last) & (s > 0))
        def _():
            back_product(m)

        @pl.when(s == 0)
        def _():
            for p in range(PIECES):
                send_cot(m, p).wait_recv()

        @pl.when(s > 0)
        def _():
            scale = squared(m)
            along = jnp.zeros((step_rows, 1), jnp.float32)
            for p in range(PIECES):
                along += jnp.sum(
                    ahead[block(m), columns(p)] * rows_in[block(m), columns(p)].astype(jnp.float32),
                    axis=-1, keepdims=True)
            pull = scale * scale * (along / width)
            for p in range(PIECES):
                values = rows_in[block(m), columns(p)].astype(jnp.float32)
                through = scale * (ahead[block(m), columns(p)] - values * pull)
                cot_out[block(m), columns(p)] = (
                    cot_in[block(m), columns(p)].astype(jnp.float32) + through).astype(jnp.bfloat16)
                send_cot(m, p).start()

        cot_side(0, m).start()
        for offset in range(1, chips):
            cot_direct(offset, m).start()
        cot_own(m).start()

        @pl.when(m > 0)
        def _():
            relay(m - 1)

    @pl.when(s == last)
    def _():
        for start in range(0, width, TILE):
            ahead[:, start:start + TILE] = lax.dot_general(
                cot_in[...], weight[start:start + TILE, :], (((1,), (1,)), ((), ())),
                preferred_element_type=jnp.float32)

    wide = 2 - blocks % 2
    paired = s >= last - 1
    lag = jnp.minimum(blocks, jnp.maximum((last - s) * 3, wide - 1))

    def step(k, carry):
        @pl.when((k < blocks) & jnp.logical_not(paired))
        def _():
            forward(k, 1)

        @pl.when((k < blocks) & paired & (k % wide == wide - 1))
        def _():
            forward(k - (wide - 1), wide)

        @pl.when(k == blocks - 1)
        def _():
            own_normed.start()
            for offset in range(1, replicas):
                send_normed(offset).start()

        @pl.when((k >= lag) & (k < lag + blocks))
        def _():
            backward(k - lag)

        return carry

    lax.fori_loop(0, 2 * blocks, step, 0)
    relay(blocks - 1)

    own_normed.wait()
    for offset in range(1, replicas):
        send_normed(offset).wait_send()
        send_normed(offset).wait_recv()
    for q in range(chunks):
        for offset in range(1, chips):
            weight_direct(offset, q).wait_send()
        for offset in range(chips):
            weight_side(offset, q).wait_send()

    def finish(m, carry):
        @pl.when(s < last)
        def _():
            for p in range(PIECES):
                send_rows(m, p).wait_send()

        @pl.when(s > 0)
        def _():
            for p in range(PIECES):
                send_cot(m, p).wait_send()

        cot_own(m).wait()
        for offset in range(1, chips):
            cot_direct(offset, m).wait_send()
        for offset in range(chips):
            cot_side(offset, m).wait_send()
            cot_side(offset, m).wait_recv()
        return carry

    lax.fori_loop(0, blocks, finish, 0)


def gradient_kernel(normed_ref, cot_ref, gradient_ref, flipped):
    @pl.when(pl.program_id(0) == 0)
    def _():
        flipped[...] = normed_ref[...].T

    gradient_ref[...] = jnp.dot(flipped[...], cot_ref[...], preferred_element_type=jnp.float32)


def local(sections, replicas, stream_in, sample_ids, epoch_buffer, layer_weight, top_cotangent):
    total, width = stream_in.shape
    blocks = sample_ids.shape[1]
    shard = layer_weight.shape[1]
    chunks = max(1, min(4, shard // 128))
    chips = replicas // 2
    dma = pltpu.SemaphoreType.DMA
    vmem = pl.BlockSpec(memory_space=pltpu.VMEM)
    anywhere = pl.BlockSpec(memory_space=pl.ANY)
    far = max(chips - 1, 1)
    decoded, normed_all, cot_all = pl.pallas_call(
        functools.partial(relay_kernel, sections, replicas, blocks),
        out_shape=(
            jax.ShapeDtypeStruct((total, width), jnp.bfloat16),
            jax.ShapeDtypeStruct((replicas * total, shard), jnp.bfloat16),
            jax.ShapeDtypeStruct((replicas * total, width), jnp.bfloat16),
        ),
        in_specs=[pl.BlockSpec(memory_space=pltpu.SMEM)] + [anywhere] * 4,
        out_specs=(vmem, anywhere, anywhere),
        scratch_shapes=[
            pltpu.VMEM((width, width), jnp.bfloat16),
            pltpu.VMEM((total, width), jnp.bfloat16),
            pltpu.VMEM((total, width), jnp.bfloat16),
            pltpu.VMEM((total, width), jnp.bfloat16),
            pltpu.VMEM((total, width), jnp.bfloat16),
            pltpu.VMEM((total, width), jnp.float32),
            pltpu.VMEM((total, width), jnp.float32),
            pltpu.VMEM(epoch_buffer.shape[1:], jnp.bfloat16),
            dma((5,)),
            dma((far, chunks)), dma((far, chunks)), dma((chips, chunks)), dma((chips, chunks)),
            dma((blocks, PIECES)), dma((blocks, PIECES)), dma((blocks, PIECES)), dma((blocks, PIECES)),
            dma((replicas - 1,)), dma((replicas - 1,)),
            dma((far, blocks)), dma((far, blocks)), dma((chips, blocks)), dma((chips, blocks)),
            dma((blocks,)),
        ],
        compiler_params=pltpu.CompilerParams(
            collective_id=0, has_side_effects=True, vmem_limit_bytes=60 * 1024 * 1024),
    )(sample_ids, epoch_buffer, stream_in, layer_weight, top_cotangent)
    gradient = pl.pallas_call(
        gradient_kernel,
        grid=(width // TILE,),
        out_shape=jax.ShapeDtypeStruct((shard, width), jnp.float32),
        in_specs=[
            pl.BlockSpec((replicas * total, shard), lambda j: (0, 0)),
            pl.BlockSpec((replicas * total, TILE), lambda j: (0, j)),
        ],
        out_specs=pl.BlockSpec((shard, TILE), lambda j: (0, j)),
        scratch_shapes=[pltpu.VMEM((shard, replicas * total), jnp.bfloat16)],
        compiler_params=pltpu.CompilerParams(vmem_limit_bytes=60 * 1024 * 1024),
    )(normed_all, cot_all)
    return (decoded[None], gradient[None])


def solution(mesh):
    in_specs = (
        P("dp", None),
        P("dp", None),
        P("section", "dp", None, None),
        P("section", "dp", None),
        P("dp", None),
    )
    out_specs = (P("section", "dp", None), P("section", "dp", None))
    body = functools.partial(local, mesh.shape["section"], mesh.shape["dp"])
    return jax.shard_map(body, mesh=mesh, in_specs=in_specs, out_specs=out_specs, check_vma=False)
```

```python
import functools

import jax
import jax.numpy as jnp
from jax import lax
from jax.experimental import pallas as pl
from jax.experimental.pallas import tpu as pltpu
from jax.sharding import PartitionSpec as P

epsilon = 1e-05
TILE = 512
PIECES = 2


def relay_kernel(sections, replicas, blocks, ids_ref, epoch_ref, stream_ref, weight_whole, top_ref,
                 decoded_ref, normed_all, cot_all,
                 weight, rows_in, normed, cot_in, cot_out, product, ahead, epoch,
                 load_sem, w_send, w_recv, w_side_send, w_side_recv,
                 x_send, x_recv, g_send, g_recv, n_send, n_recv,
                 c_send, c_recv, c_side_send, c_side_recv, own_sem):
    s = lax.axis_index("section")
    me = lax.axis_index("dp")
    last = sections - 1
    chips = replicas // 2
    chip, core = me // 2, lax.rem(me, 2)
    sibling = chip * 2 + 1 - core
    total, width = rows_in.shape
    step_rows = total // blocks
    weight_ref = weight_whole.at[0]
    shard = weight_ref.shape[0]
    span = width // PIECES
    chunks = w_send.shape[1]
    piece = shard // chunks
    after, before = lax.rem(s + 1, sections), lax.rem(s + last, sections)

    def peer(offset):
        return lax.rem(chip + offset, chips) * 2 + core

    def source(offset):
        return lax.rem(chip + chips - offset, chips) * 2

    def block(m):
        return pl.ds(pl.multiple_of(m * step_rows, step_rows), step_rows)

    def remote(src, dst, send, recv, **where):
        return pltpu.make_async_remote_copy(
            src_ref=src, dst_ref=dst, send_sem=send, recv_sem=recv,
            device_id=where, device_id_type=pl.DeviceIdType.MESH)

    barrier = pltpu.get_barrier_semaphore()

    def greet(**where):
        pl.semaphore_signal(barrier, inc=1, device_id=where, device_id_type=pl.DeviceIdType.MESH)

    for offset in range(1, replicas):
        greet(dp=lax.rem(me + offset, replicas))

    @pl.when(s < last)
    def _():
        greet(section=after)

    @pl.when(s > 0)
    def _():
        greet(section=before)

    stream_load = pltpu.make_async_copy(stream_ref, rows_in, load_sem.at[0])
    top_load = pltpu.make_async_copy(top_ref, cot_in, load_sem.at[1])
    shard_load = pltpu.make_async_copy(
        weight_ref, weight.at[pl.ds(pl.multiple_of(me * shard, shard), shard)], load_sem.at[2])
    shard_load.start()
    epoch_load = pltpu.make_async_copy(epoch_ref.at[0], epoch, load_sem.at[4])

    @pl.when(s == 0)
    def _():
        stream_load.start()

    @pl.when(s == last)
    def _():
        top_load.start()

    pl.semaphore_wait(
        barrier, replicas - 1 + jnp.minimum(s, 1) + jnp.minimum(last - s, 1))

    def weight_rows(owner, q):
        return weight.at[pl.ds(pl.multiple_of(owner * shard + q * piece, piece), piece)]

    def weight_direct(offset, q):
        return remote(weight_ref.at[pl.ds(q * piece, piece)], weight_rows(me, q),
                      w_send.at[offset - 1, q], w_recv.at[offset - 1, q], dp=peer(offset))

    def weight_side(offset, q):
        if offset == 0:
            src = weight_ref.at[pl.ds(q * piece, piece)]
        else:
            src = weight_rows(source(offset) + core, q)
        return remote(src, weight_rows(source(offset) + core, q),
                      w_side_send.at[offset, q], w_side_recv.at[offset, q], dp=sibling)

    for q in range(chunks):
        for offset in range(1, chips):
            weight_direct(offset, q).start()
        weight_side(0, q).start()
    epoch_load.start()
    def absorb(first, depth):
        @pl.when(s == 0)
        def _():
            lanes = pl.ds(pl.multiple_of(first, depth), depth)
            for start in range(0, width, TILE):
                product[:, start:start + TILE] += jnp.dot(
                    rows_in[:, lanes], weight[lanes, start:start + TILE],
                    preferred_element_type=jnp.float32)

    @pl.when(s == 0)
    def _():
        stream_load.wait()
        product[...] = jnp.zeros_like(product)

    shard_load.wait()
    absorb(me * shard, shard)
    for q in range(chunks):
        weight_side(0, q).wait_recv()
    absorb(sibling * shard, shard)
    for q in range(chunks):
        for offset in range(1, chips):
            weight_direct(offset, q).wait_recv()
            weight_side(offset, q).start()
        for offset in range(1, chips):
            absorb((source(offset) + core) * shard + q * piece, piece)
        for offset in range(1, chips):
            weight_side(offset, q).wait_recv()
            absorb((source(offset) + 1 - core) * shard + q * piece, piece)

    @pl.when(s == last)
    def _():
        top_load.wait()

    epoch_load.wait()

    def columns(p):
        return slice(p * span, (p + 1) * span)

    def send_rows(m, p):
        return remote(decoded_ref.at[block(m), columns(p)], rows_in.at[block(m), columns(p)],
                      x_send.at[m, p], x_recv.at[m, p], section=after)

    def send_cot(m, p):
        return remote(cot_out.at[block(m), columns(p)], cot_in.at[block(m), columns(p)],
                      g_send.at[m, p], g_recv.at[m, p], section=before)

    def send_normed(offset):
        other = lax.rem(me + offset, replicas)
        return remote(normed.at[:, pl.ds(pl.multiple_of(other * shard, shard), shard)],
                      normed_all.at[pl.ds(pl.multiple_of(me * total, total), total)],
                      n_send.at[offset - 1], n_recv.at[offset - 1], dp=other)

    own_normed = pltpu.make_async_copy(
        normed.at[:, pl.ds(pl.multiple_of(me * shard, shard), shard)],
        normed_all.at[pl.ds(pl.multiple_of(me * total, total), total)], load_sem.at[3])

    def cot_rows(owner, m):
        return cot_all.at[pl.ds(pl.multiple_of(owner * total + m * step_rows, step_rows), step_rows)]

    def cot_direct(offset, m):
        return remote(cot_in.at[block(m)], cot_rows(me, m),
                      c_send.at[offset - 1, m], c_recv.at[offset - 1, m], dp=peer(offset))

    def cot_side(offset, m):
        owner = source(offset) + core
        src = cot_in.at[block(m)] if offset == 0 else cot_rows(owner, m)
        return remote(src, cot_rows(owner, m),
                      c_side_send.at[offset, m], c_side_recv.at[offset, m], dp=sibling)

    def cot_own(m):
        return pltpu.make_async_copy(cot_in.at[block(m)], cot_rows(me, m), own_sem.at[m])

    def relay(m):
        for offset in range(1, chips):
            cot_direct(offset, m).wait_recv()
            cot_side(offset, m).start()

    def squared(m):
        total_squares = jnp.zeros((step_rows, 1), jnp.float32)
        for p in range(PIECES):
            part = rows_in[block(m), columns(p)].astype(jnp.float32)
            total_squares += jnp.sum(part * part, axis=-1, keepdims=True)
        return lax.rsqrt(total_squares / width + epsilon)

    def forward(m, count):
        group = pl.ds(pl.multiple_of(m * step_rows, step_rows), count * step_rows)

        @pl.when(s > 0)
        def _():
            for p in range(PIECES):
                for i in range(count):
                    send_rows(m + i, p).wait_recv()
                piece_rows = rows_in[group, columns(p)]
                for start in range(0, width, TILE):
                    part = jnp.dot(piece_rows, weight[columns(p), start:start + TILE],
                                   preferred_element_type=jnp.float32)
                    if p > 0:
                        part += product[group, start:start + TILE]
                    product[group, start:start + TILE] = part

        for i in range(count):
            scale = squared(m + i)
            squares = jnp.zeros((step_rows, 1), jnp.float32)
            for p in range(PIECES):
                values = rows_in[block(m + i), columns(p)].astype(jnp.float32)
                part = values + scale * product[block(m + i), columns(p)]
                product[block(m + i), columns(p)] = part
                squares += jnp.sum(part * part, axis=-1, keepdims=True)
            bound = 2.0 * jnp.sqrt(squares / width + epsilon)
            entry = ids_ref[0, m + i]
            for p in range(PIECES):
                base = epoch[entry, :, columns(p)].astype(jnp.float32)
                delta = jnp.clip(product[block(m + i), columns(p)] - base, -bound, bound).astype(
                    jnp.bfloat16)
                decoded_ref[block(m + i), columns(p)] = (
                    base + delta.astype(jnp.float32)).astype(jnp.bfloat16)

                @pl.when(s < last)
                def _():
                    send_rows(m + i, p).start()

            for p in range(PIECES):
                values = rows_in[block(m + i), columns(p)].astype(jnp.float32)
                normed[block(m + i), columns(p)] = (values * scale).astype(jnp.bfloat16)

    def back_product(m):
        for p in range(PIECES):
            send_cot(m, p).wait_recv()
            incoming = cot_in[block(m), columns(p)]
            for start in range(0, width, TILE):
                part = lax.dot_general(incoming, weight[start:start + TILE, columns(p)],
                                       (((1,), (1,)), ((), ())), preferred_element_type=jnp.float32)
                if p > 0:
                    part += ahead[block(m), start:start + TILE]
                ahead[block(m), start:start + TILE] = part

    def backward(m):
        @pl.when((s < last) & (s > 0))
        def _():
            back_product(m)

        @pl.when(s == 0)
        def _():
            for p in range(PIECES):
                send_cot(m, p).wait_recv()

        @pl.when(s > 0)
        def _():
            scale = squared(m)
            along = jnp.zeros((step_rows, 1), jnp.float32)
            for p in range(PIECES):
                along += jnp.sum(
                    ahead[block(m), columns(p)] * rows_in[block(m), columns(p)].astype(jnp.float32),
                    axis=-1, keepdims=True)
            pull = scale * scale * (along / width)
            for p in range(PIECES):
                values = rows_in[block(m), columns(p)].astype(jnp.float32)
                through = scale * (ahead[block(m), columns(p)] - values * pull)
                cot_out[block(m), columns(p)] = (
                    cot_in[block(m), columns(p)].astype(jnp.float32) + through).astype(jnp.bfloat16)
                send_cot(m, p).start()

        cot_side(0, m).start()
        for offset in range(1, chips):
            cot_direct(offset, m).start()
        cot_own(m).start()

        @pl.when(m > 0)
        def _():
            relay(m - 1)

    @pl.when(s == last)
    def _():
        for start in range(0, width, TILE):
            ahead[:, start:start + TILE] = lax.dot_general(
                cot_in[...], weight[start:start + TILE, :], (((1,), (1,)), ((), ())),
                preferred_element_type=jnp.float32)

    wide = 2 - blocks % 2
    paired = s >= last - 1
    lag = jnp.minimum(blocks, jnp.maximum((last - s) * 3, wide - 1))

    def step(k, carry):
        @pl.when((k < blocks) & jnp.logical_not(paired))
        def _():
            forward(k, 1)

        @pl.when((k < blocks) & paired & (k % wide == wide - 1))
        def _():
            forward(k - (wide - 1), wide)

        @pl.when(k == blocks - 1)
        def _():
            own_normed.start()
            for offset in range(1, replicas):
                send_normed(offset).start()

        @pl.when((k >= lag) & (k < lag + blocks))
        def _():
            backward(k - lag)

        return carry

    lax.fori_loop(0, 2 * blocks, step, 0)
    relay(blocks - 1)

    own_normed.wait()
    for offset in range(1, replicas):
        send_normed(offset).wait_send()
        send_normed(offset).wait_recv()
    for q in range(chunks):
        for offset in range(1, chips):
            weight_direct(offset, q).wait_send()
        for offset in range(chips):
            weight_side(offset, q).wait_send()

    def finish(m, carry):
        @pl.when(s < last)
        def _():
            for p in range(PIECES):
                send_rows(m, p).wait_send()

        @pl.when(s > 0)
        def _():
            for p in range(PIECES):
                send_cot(m, p).wait_send()

        cot_own(m).wait()
        for offset in range(1, chips):
            cot_direct(offset, m).wait_send()
        for offset in range(chips):
            cot_side(offset, m).wait_send()
            cot_side(offset, m).wait_recv()
        return carry

    lax.fori_loop(0, blocks, finish, 0)


def gradient_kernel(normed_ref, cot_ref, gradient_ref, flipped):
    @pl.when(pl.program_id(0) == 0)
    def _():
        flipped[...] = normed_ref[...].T

    gradient_ref[...] = jnp.dot(flipped[...], cot_ref[...], preferred_element_type=jnp.float32)


def local(sections, replicas, stream_in, sample_ids, epoch_buffer, layer_weight, top_cotangent):
    total, width = stream_in.shape
    blocks = sample_ids.shape[1]
    shard = layer_weight.shape[1]
    chunks = max(1, min(4, shard // 128))
    chips = replicas // 2
    dma = pltpu.SemaphoreType.DMA
    vmem = pl.BlockSpec(memory_space=pltpu.VMEM)
    anywhere = pl.BlockSpec(memory_space=pl.ANY)
    far = max(chips - 1, 1)
    decoded, normed_all, cot_all = pl.pallas_call(
        functools.partial(relay_kernel, sections, replicas, blocks),
        out_shape=(
            jax.ShapeDtypeStruct((total, width), jnp.bfloat16),
            jax.ShapeDtypeStruct((replicas * total, shard), jnp.bfloat16),
            jax.ShapeDtypeStruct((replicas * total, width), jnp.bfloat16),
        ),
        in_specs=[pl.BlockSpec(memory_space=pltpu.SMEM)] + [anywhere] * 4,
        out_specs=(vmem, anywhere, anywhere),
        scratch_shapes=[
            pltpu.VMEM((width, width), jnp.bfloat16),
            pltpu.VMEM((total, width), jnp.bfloat16),
            pltpu.VMEM((total, width), jnp.bfloat16),
            pltpu.VMEM((total, width), jnp.bfloat16),
            pltpu.VMEM((total, width), jnp.bfloat16),
            pltpu.VMEM((total, width), jnp.float32),
            pltpu.VMEM((total, width), jnp.float32),
            pltpu.VMEM(epoch_buffer.shape[1:], jnp.bfloat16),
            dma((5,)),
            dma((far, chunks)), dma((far, chunks)), dma((chips, chunks)), dma((chips, chunks)),
            dma((blocks, PIECES)), dma((blocks, PIECES)), dma((blocks, PIECES)), dma((blocks, PIECES)),
            dma((replicas - 1,)), dma((replicas - 1,)),
            dma((far, blocks)), dma((far, blocks)), dma((chips, blocks)), dma((chips, blocks)),
            dma((blocks,)),
        ],
        compiler_params=pltpu.CompilerParams(
            collective_id=0, has_side_effects=True, vmem_limit_bytes=60 * 1024 * 1024),
    )(sample_ids, epoch_buffer, stream_in, layer_weight, top_cotangent)
    gradient = pl.pallas_call(
        gradient_kernel,
        grid=(width // TILE,),
        out_shape=jax.ShapeDtypeStruct((shard, width), jnp.float32),
        in_specs=[
            pl.BlockSpec((replicas * total, shard), lambda j: (0, 0)),
            pl.BlockSpec((replicas * total, TILE), lambda j: (0, j)),
        ],
        out_specs=pl.BlockSpec((shard, TILE), lambda j: (0, j)),
        scratch_shapes=[pltpu.VMEM((shard, replicas * total), jnp.bfloat16)],
        compiler_params=pltpu.CompilerParams(vmem_limit_bytes=60 * 1024 * 1024),
    )(normed_all, cot_all)
    return (decoded[None], gradient[None])


def solution(mesh):
    in_specs = (
        P("dp", None),
        P("dp", None),
        P("section", "dp", None, None),
        P("section", "dp", None),
        P("dp", None),
    )
    out_specs = (P("section", "dp", None), P("section", "dp", None))
    body = functools.partial(local, mesh.shape["section"], mesh.shape["dp"])
    return jax.shard_map(body, mesh=mesh, in_specs=in_specs, out_specs=out_specs, check_vma=False)
```
